32 devices in a mesh: nodes: 8 (over z, y), rep: 4 (over x, core).
Axes of the slice: x: 2, y: 2, z: 4, core: 2. Of those that a mesh axis runs over, the one named last changes fastest.
Arguments:
- queries: bfloat16 [4, 4096, 1024], P('rep', 'nodes'), may hold values from -9 to 9
- keys: bfloat16 [4, 4096, 1024], P('rep', 'nodes'), may hold values from -9 to 9
- values: bfloat16 [4, 4096, 1024], P('rep', 'nodes'), may hold values from -6 to 6
- grad_out: bfloat16 [4, 4096, 1024], P('rep', 'nodes'), may hold values from -6 to 6
- w_out: bfloat16 [1024, 1024], replicated, may hold values from -0.1875 to 0.1875
- cluster_id: int32 [4, 4096], P('rep', 'nodes'), may hold values from 0 to 31, as said below
Outputs:
- grad_queries: bfloat16 [4, 4096, 1024], P('rep', 'nodes')
- grad_keys: bfloat16 [4, 4096, 1024], P('rep', 'nodes')
- grad_values: bfloat16 [4, 4096, 1024], P('rep', 'nodes')
- grad_w_out: float32 [1024, 1024], P('nodes')
The draws below stay inside these ranges and needn't reach their ends.
Inputs may be any that keep to these rules, and one draw needn't show every extreme that they name: `cluster_id`: cluster c of a window is owned by index c // 4 of the nodes axis. The 512 nodes of one device name clusters of every owner, exactly 64 nodes for each owner. Clusters differ in size and may be empty.
All inputs are finite; a program needn't handle non-finite values.
Results may differ from the reference program's by a relative error of at most 0.013.
The reference program's roundings to bfloat16 on the way count: a program that leaves them out, or rounds other values in their place, can miss the bound.
Values may be sent and summed in bfloat16 or wider, within the bound.
A program may use at most 128 MiB of HBM per device.

```python
import math
import jax
import jax.numpy as jnp
from jax import lax

D = 1024
HEADS = 8
HEAD_DIM = 128
CL_DEV = 4
NODE_DEV = 512
BUCKET = 64
NODES_G = 4096
N_NODES = 8
N_REP = 4


def draw_queries(key, part):
    base_rows = jnp.clip(jax.random.normal(jax.random.fold_in(key, 11), (N_REP, NODE_DEV * N_NODES, D), jnp.float32), -6.0, 6.0)
    return base_rows.astype(jnp.bfloat16)


def draw_keys(key, part):
    base_rows = jnp.clip(jax.random.normal(jax.random.fold_in(key, 12), (N_REP, NODE_DEV * N_NODES, D), jnp.float32), -6.0, 6.0)
    return base_rows.astype(jnp.bfloat16)


def draw_cluster_id(key, part):
    bucket = NODE_DEV // N_NODES

    def window_ids(window_key):
        kept = jax.random.randint(jax.random.fold_in(window_key, 1), (N_NODES,), 1, CL_DEV + 1).astype(jnp.int32)
        kept = kept.at[N_NODES - 1].set(CL_DEV)

        def device_ids(device_rank):
            device_key = jax.random.fold_in(window_key, device_rank + 100)
            slot_order = jax.random.permutation(jax.random.fold_in(device_key, 3), NODE_DEV).astype(jnp.int32)
            owner_of = (slot_order // bucket).astype(jnp.int32)
            raw_sub = jax.random.randint(jax.random.fold_in(device_key, 4), (NODE_DEV,), 0, 1048576).astype(jnp.int32)
            sub_cluster = jnp.remainder(raw_sub, kept[owner_of]).astype(jnp.int32)
            return (owner_of * CL_DEV + sub_cluster).astype(jnp.int32)
        return jax.vmap(device_ids)(jnp.arange(N_NODES, dtype=jnp.int32)).reshape(-1)
    window_keys = jax.vmap(lambda window: jax.random.fold_in(key, window))(jnp.arange(N_REP, dtype=jnp.int32))
    return jax.vmap(window_ids)(window_keys)


def strengthened(values, rng, source, target, shards_of, factor):
    owner, partner = [(jnp.arange(values.shape[position]) // (values.shape[position] // shards_of)).reshape([-1 if axis == position else 1 for axis in range(values.ndim)]) for position in (source, target)]
    chosen = jax.random.permutation(rng, shards_of)[partner]
    strong = (owner == chosen) | (owner == (partner + shards_of // 2) % shards_of)
    return jnp.where(strong, factor * values, values)


def steps_of(stream_key, shape, pieces, smallest, high):
    loudness, own = 1.0, jax.random.fold_in(stream_key, 6)
    for position, parts in pieces:
        draws = jnp.exp(jax.random.uniform(jax.random.fold_in(own, position), (parts,), jnp.float32, smallest / len(pieces), high / len(pieces)))
        loudness = loudness * jnp.repeat(draws, shape[position] // parts).reshape([-1 if axis == position else 1 for axis in range(len(shape))])
    return loudness


def bell_draw(own_key, shape, spread, most, split=(), kind=jnp.bfloat16):
    entries = spread * jax.random.normal(own_key, shape, jnp.float32)
    if split:
        entries = entries * steps_of(own_key, shape, split, -0.22, 0.18)
    return jnp.clip(entries, -most, most).astype(kind)


def heavy_noise(key, dims, scale, bound, pieces, heavy, held_as=jnp.bfloat16):
    values = scale * jax.random.normal(key, dims, jnp.float32)
    if pieces:
        values = values * steps_of(key, dims, pieces, -0.22, 0.18)
    return jnp.clip(strengthened(values, jax.random.fold_in(key, 3), *heavy), -bound, bound).astype(held_as)


def setup_inputs(seed: int = 0) -> dict:
    streams_of = jax.random.split(jax.random.key(seed), 7)
    return {
        "queries": draw_queries(jax.random.fold_in(streams_of[6], 71), 0),
        "keys": draw_keys(jax.random.fold_in(streams_of[6], 71), 0),
        "values": bell_draw(streams_of[2], (N_REP, NODES_G, D), 1.0, 6.0, ((0, 4), (1, 8))),
        "grad_out": heavy_noise(streams_of[3], (N_REP, NODES_G, D), 1.0, 6.0, ((0, 4), (1, 8)), (1, 2, 8, 2.0)),
        "w_out": bell_draw(streams_of[4], (D, D), D ** -0.5, 0.1875),
        "cluster_id": draw_cluster_id(jax.random.fold_in(streams_of[6], 71), 0),
    }


big_negative = -1e+30

def head_grads(query_rows, key_rows, value_rows, grad_rows, tag_rows, score_scale):
    scores = lax.dot_general(query_rows, key_rows, (((1,), (1,)), ((), ())), preferred_element_type=jnp.float32) * score_scale
    allowed = (tag_rows[:, None] == tag_rows[None, :]) & (tag_rows[None, :] > 0)
    scores = jnp.where(allowed, scores, big_negative)
    highest = lax.optimization_barrier(jnp.max(scores, axis=1, keepdims=True))
    weights = jnp.exp(scores - highest)
    softmax_rows = weights / lax.optimization_barrier(jnp.sum(weights, axis=1, keepdims=True))
    softmax_low = softmax_rows.astype(jnp.bfloat16)
    attended = jnp.dot(softmax_low, value_rows, preferred_element_type=jnp.float32).astype(jnp.bfloat16)
    delta_rows = lax.optimization_barrier(jnp.sum(grad_rows.astype(jnp.float32) * attended.astype(jnp.float32), axis=1, keepdims=True))
    grad_softmax = lax.dot_general(grad_rows, value_rows, (((1,), (1,)), ((), ())), preferred_element_type=jnp.float32)
    grad_scores = (softmax_rows * (grad_softmax - delta_rows) * score_scale).astype(jnp.bfloat16)
    grad_query = jnp.dot(grad_scores, key_rows, preferred_element_type=jnp.float32).astype(jnp.bfloat16)
    grad_key = lax.dot_general(grad_scores, query_rows, (((0,), (0,)), ((), ())), preferred_element_type=jnp.float32).astype(jnp.bfloat16)
    grad_value = lax.dot_general(softmax_low, grad_rows, (((0,), (0,)), ((), ())), preferred_element_type=jnp.float32).astype(jnp.bfloat16)
    return (grad_query, grad_key, grad_value, attended)

def all_heads(query_all, key_all, value_all, grad_all, tag_all, score_scale):
    collected = [[], [], [], []]
    for head_index in range(query_all.shape[1]):
        outputs = head_grads(query_all[:, head_index], key_all[:, head_index], value_all[:, head_index], grad_all[:, head_index], tag_all[:, head_index], score_scale)
        for member in range(4):
            collected[member].append(outputs[member])
    return tuple((jnp.stack(pieces_list, axis=1) for pieces_list in collected))

def reference(queries, keys, values, grad_out, w_out, cluster_id):
    buffer_rows = N_NODES * BUCKET
    score_scale = 1.0 / math.sqrt(HEAD_DIM)
    nodes_window = queries.shape[1]
    model_width = queries.shape[2]
    head_shape = (buffer_rows, HEADS, HEAD_DIM)
    grad_attended = jnp.dot(grad_out.reshape(-1, model_width), w_out, preferred_element_type=jnp.float32).astype(jnp.bfloat16).reshape(grad_out.shape)
    results_all = [[], [], [], []]
    weight_total = jnp.zeros((model_width, model_width), jnp.float32)
    for window in range(N_REP):
        owner_ids = (cluster_id[window] // CL_DEV).astype(jnp.int32)
        sub_ids = (cluster_id[window] - owner_ids * CL_DEV).astype(jnp.int32)
        sort_order = jnp.argsort(owner_ids, stable=True).astype(jnp.int32)
        owner_range = jnp.arange(N_NODES, dtype=jnp.int32)
        counts = lax.optimization_barrier(jnp.sum((owner_ids[None, :] == owner_range[:, None]).astype(jnp.int32), axis=1)).astype(jnp.int32)
        starts = (jnp.cumsum(counts) - counts).astype(jnp.int32)

        def sorted_padded(array):
            tail = jnp.zeros((buffer_rows,) + array.shape[1:], array.dtype)
            return jnp.concatenate([array[sort_order], tail], axis=0)
        sorted_sets = [sorted_padded(queries[window]), sorted_padded(keys[window]), sorted_padded(values[window]), sorted_padded(grad_attended[window])]
        sorted_tag = sorted_padded(sub_ids + 1)
        sorted_node = sorted_padded(jnp.arange(nodes_window, dtype=jnp.int32))
        initial = tuple((jnp.zeros((nodes_window + 1, model_width), jnp.bfloat16) for member in range(4)))

        def owner_step(carry, owner):
            first_row = starts[owner]
            live = jnp.arange(buffer_rows, dtype=jnp.int32) < counts[owner]
            blocks = []
            for array in sorted_sets:
                taken = lax.dynamic_slice_in_dim(array, first_row, buffer_rows, 0)
                blocks.append(jnp.where(live[:, None], taken, jnp.zeros_like(taken)).reshape(head_shape))
            tag_line = jnp.where(live, lax.dynamic_slice_in_dim(sorted_tag, first_row, buffer_rows, 0), 0).astype(jnp.int32)
            tag_all = jnp.broadcast_to(tag_line[:, None], (buffer_rows, HEADS))
            target = jnp.where(live, lax.dynamic_slice_in_dim(sorted_node, first_row, buffer_rows, 0), nodes_window).astype(jnp.int32)
            results = all_heads(blocks[0], blocks[1], blocks[2], blocks[3], tag_all, score_scale)
            updated = tuple((held.at[target].set(result.reshape(buffer_rows, model_width)) for held, result in zip(carry, results)))
            return (updated, None)
        final, unused = lax.scan(owner_step, initial, owner_range)
        for member in range(4):
            results_all[member].append(final[member][:nodes_window])
        weight_total = weight_total + lax.dot_general(grad_out[window], final[3][:nodes_window], (((0,), (0,)), ((), ())), preferred_element_type=jnp.float32)
    norm_factor = 1.0 / math.sqrt(N_REP * nodes_window)
    grad_queries = jnp.stack(results_all[0], axis=0)
    grad_keys = jnp.stack(results_all[1], axis=0)
    grad_values = jnp.stack(results_all[2], axis=0)
    return (grad_queries, grad_keys, grad_values, weight_total * norm_factor)
```

```python
import functools
import math

import jax
import jax.numpy as jnp
from jax import lax
from jax.experimental import pallas as pl
from jax.experimental.pallas import tpu as pltpu
from jax.sharding import PartitionSpec as P

HEAD_DIM = 128
CL_DEV = 4
GROUP_HEADS = 2
TAG_LANES = 128
MESH = pl.DeviceIdType.MESH


big_negative = -1e30


def head_grads(query_rows, key_rows, value_rows, grad_rows, tag_rows, score_scale):
    scores = (
        lax.dot_general(
            query_rows, key_rows, (((1,), (1,)), ((), ())), preferred_element_type=jnp.float32
        )
        * score_scale
    )
    allowed = (tag_rows[:, None] == tag_rows[None, :]) & (tag_rows[None, :] > 0)
    scores = jnp.where(allowed, scores, big_negative)
    highest = jnp.max(scores, axis=1, keepdims=True)
    weights = jnp.exp(scores - highest)
    softmax_rows = weights / jnp.sum(weights, axis=1, keepdims=True)
    softmax_low = softmax_rows.astype(jnp.bfloat16)
    attended = jnp.dot(softmax_low, value_rows, preferred_element_type=jnp.float32).astype(
        jnp.bfloat16
    )
    delta_rows = jnp.sum(
        grad_rows.astype(jnp.float32) * attended.astype(jnp.float32), axis=1, keepdims=True
    )
    grad_softmax = lax.dot_general(
        grad_rows, value_rows, (((1,), (1,)), ((), ())), preferred_element_type=jnp.float32
    )
    grad_scores = (softmax_rows * (grad_softmax - delta_rows) * score_scale).astype(jnp.bfloat16)
    grad_query = jnp.dot(grad_scores, key_rows, preferred_element_type=jnp.float32).astype(
        jnp.bfloat16
    )
    grad_key = lax.dot_general(
        grad_scores, query_rows, (((0,), (0,)), ((), ())), preferred_element_type=jnp.float32
    ).astype(jnp.bfloat16)
    grad_value = lax.dot_general(
        softmax_low, grad_rows, (((0,), (0,)), ((), ())), preferred_element_type=jnp.float32
    ).astype(jnp.bfloat16)
    return (grad_query, grad_key, grad_value, attended)


def all_heads(query_all, key_all, value_all, grad_all, tag_all, score_scale):
    collected = [[], [], [], []]
    for head_index in range(query_all.shape[1]):
        outputs = head_grads(
            query_all[:, head_index],
            key_all[:, head_index],
            value_all[:, head_index],
            grad_all[:, head_index],
            tag_all[:, head_index],
            score_scale,
        )
        for member in range(4):
            collected[member].append(outputs[member])
    return tuple((jnp.stack(pieces_list, axis=1) for pieces_list in collected))


def local_plain(queries, keys, values, grad_out, w_out, cluster_id):
    node_count = lax.axis_size("nodes")
    rows_here = queries.shape[1]
    model_width = queries.shape[2]
    head_count = model_width // HEAD_DIM
    bucket = rows_here // node_count
    buffer_rows = node_count * bucket
    head_shape = (buffer_rows, head_count, HEAD_DIM)
    score_scale = 1.0 / math.sqrt(HEAD_DIM)
    norm_factor = 1.0 / math.sqrt(lax.axis_size("rep") * node_count * rows_here)
    cluster_ids = cluster_id[0]
    owner_ids = cluster_ids // CL_DEV
    sub_ids = cluster_ids - owner_ids * CL_DEV
    owner_table = (owner_ids[:, None] == jnp.arange(node_count, dtype=jnp.int32)[None, :]).astype(
        jnp.float32
    )
    row_numbers = jnp.arange(rows_here, dtype=jnp.int32)
    earlier = (row_numbers[:, None] > row_numbers[None, :]).astype(jnp.float32)
    before = jnp.dot(earlier, owner_table, precision=lax.Precision.HIGHEST)
    rank_in_bucket = jnp.sum(before * owner_table, axis=1).astype(jnp.int32)
    slot_index = owner_ids * bucket + rank_in_bucket

    def to_buffer(rows):
        return jnp.zeros((buffer_rows,) + rows.shape[1:], rows.dtype).at[slot_index].set(rows)

    tag_column = to_buffer((sub_ids + 1).astype(jnp.bfloat16))
    tag_grid = jnp.broadcast_to(tag_column[:, None], (buffer_rows, head_count))
    query_local = queries[0]
    key_local = keys[0]
    value_local = values[0]
    grad_local = grad_out[0]
    arrived = (
        lax.all_to_all(to_buffer(query_local), "nodes", split_axis=0, concat_axis=0, tiled=True),
        lax.all_to_all(to_buffer(key_local), "nodes", split_axis=0, concat_axis=0, tiled=True),
        lax.all_to_all(to_buffer(value_local), "nodes", split_axis=0, concat_axis=0, tiled=True),
        lax.all_to_all(to_buffer(grad_local), "nodes", split_axis=0, concat_axis=0, tiled=True),
        lax.all_to_all(tag_grid, "nodes", split_axis=0, concat_axis=0, tiled=True),
    )
    query_recv, key_recv, value_recv, grad_recv, tag_recv = arrived
    grad_attended = jnp.dot(grad_recv, w_out, preferred_element_type=jnp.float32).astype(
        jnp.bfloat16
    )
    results = all_heads(
        query_recv.reshape(head_shape),
        key_recv.reshape(head_shape),
        value_recv.reshape(head_shape),
        grad_attended.reshape(head_shape),
        tag_recv,
        score_scale,
    )
    flattened = [result.reshape(buffer_rows, model_width) for result in results]
    returned = (
        lax.all_to_all(flattened[0], "nodes", split_axis=0, concat_axis=0, tiled=True),
        lax.all_to_all(flattened[1], "nodes", split_axis=0, concat_axis=0, tiled=True),
        lax.all_to_all(flattened[2], "nodes", split_axis=0, concat_axis=0, tiled=True),
    )
    grad_query = returned[0][slot_index]
    grad_key = returned[1][slot_index]
    grad_value = returned[2][slot_index]
    attended_rows = flattened[3]
    row_share = lax.psum_scatter(
        lax.dot_general(
            grad_recv, attended_rows, (((0,), (0,)), ((), ())), preferred_element_type=jnp.float32
        )
        * norm_factor,
        "nodes",
        scatter_dimension=0,
        tiled=True,
    )
    grad_weight = lax.psum(row_share.astype(jnp.bfloat16), "rep").astype(jnp.float32)
    return (grad_query[None], grad_key[None], grad_value[None], grad_weight)


def dot_rows(a, b):
    return lax.dot_general(a, b, (((0,), (0,)), ((), ())), preferred_element_type=jnp.float32)


def dot_lanes(a, b):
    return lax.dot_general(a, b, (((1,), (1,)), ((), ())), preferred_element_type=jnp.float32)


def dot(a, b):
    return jnp.dot(a, b, preferred_element_type=jnp.float32)


def layer_kernel(
    nn, rr, groups, norm_factor,
    slot_row, slot_col, tags, q_ref, k_ref, v_ref, g_ref, w_ref,
    dq_ref, dk_ref, dv_ref, dw_ref,
    perm, unperm, gsend, grecv, send, recv, ga, bias, att, bsend, brecv,
    wsend, wrecv, nsend, nrecv, fsend, frecv,
    g_ss, g_rs, in_ss, in_rs, b_ss, b_rs, w_ss, w_rs, n_ss, n_rs, f_ss, f_rs,
):
    low = jnp.bfloat16
    me = lax.axis_index("nodes")
    mr = lax.axis_index("rep")
    rows, width = q_ref.shape
    bucket = rows // nn
    gcols = width // groups
    seg = width // (nn * rr)
    scale = 1.0 / math.sqrt(HEAD_DIM)

    def ahead(d):
        return lax.rem(me + d, nn)

    def behind(d):
        return lax.rem(me + nn - d, nn)

    def rep_ahead(d):
        return lax.rem(mr + d, rr)

    def rep_behind(d):
        return lax.rem(mr + rr - d, rr)

    def g_copy(d, slot):
        peer = ahead(d)
        return pltpu.make_async_remote_copy(
            src_ref=gsend.at[peer], dst_ref=grecv.at[slot], send_sem=g_ss.at[d],
            recv_sem=g_rs.at[d], device_id={"nodes": peer}, device_id_type=MESH)

    def in_copy(g, d, slot):
        peer = ahead(d)
        return pltpu.make_async_remote_copy(
            src_ref=send.at[g, peer], dst_ref=recv.at[g, slot], send_sem=in_ss.at[g, d],
            recv_sem=in_rs.at[g, d], device_id={"nodes": peer}, device_id_type=MESH)

    def back_copy(g, d, slot):
        peer = ahead(d)
        return pltpu.make_async_remote_copy(
            src_ref=bsend.at[g, peer], dst_ref=brecv.at[g, slot], send_sem=b_ss.at[g, d],
            recv_sem=b_rs.at[g, d], device_id={"nodes": peer}, device_id_type=MESH)

    def w_copy(g, d, slot):
        peer = rep_ahead(d)
        return pltpu.make_async_remote_copy(
            src_ref=wsend.at[g, peer], dst_ref=wrecv.at[g, slot], send_sem=w_ss.at[g, d],
            recv_sem=w_rs.at[g, d], device_id={"rep": peer}, device_id_type=MESH)

    def n_copy(g, d, slot):
        peer = ahead(d)
        return pltpu.make_async_remote_copy(
            src_ref=nsend.at[g, peer], dst_ref=nrecv.at[g, slot], send_sem=n_ss.at[g, d],
            recv_sem=n_rs.at[g, d], device_id={"nodes": peer}, device_id_type=MESH)

    def f_copy(d, slot):
        peer = rep_ahead(d)
        return pltpu.make_async_remote_copy(
            src_ref=fsend, dst_ref=frecv.at[slot], send_sem=f_ss.at[d],
            recv_sem=f_rs.at[d], device_id={"rep": peer}, device_id_type=MESH)

    def each(count, act):
        def step(d, carry):
            act(d)
            return carry

        lax.fori_loop(1, count, step, 0)

    barrier = pltpu.get_barrier_semaphore()
    for d in range(1, nn):
        pl.semaphore_signal(barrier, inc=1, device_id={"nodes": ahead(d)}, device_id_type=MESH)
    for d in range(1, rr):
        pl.semaphore_signal(barrier, inc=1, device_id={"rep": rep_ahead(d)}, device_id_type=MESH)

    perm[...] = (
        lax.broadcasted_iota(jnp.int32, (rows, rows), 0) == slot_row[...]
    ).astype(jnp.float32).astype(low)
    unperm[...] = (
        lax.broadcasted_iota(jnp.int32, (rows, rows), 1) == slot_col[...]
    ).astype(jnp.float32).astype(low)

    gsend[:, :, :width] = dot(perm[...], g_ref[...]).astype(low).reshape(nn, bucket, width)
    gsend[:, :, width:] = dot(perm[...], tags[...]).astype(low).reshape(nn, bucket, TAG_LANES)
    pl.semaphore_wait(barrier, nn + rr - 2)
    each(nn, lambda d: g_copy(d, me).start())
    grecv[me] = gsend[me]

    def perm_send(g):
        cols = pl.ds(pl.multiple_of(g * gcols, HEAD_DIM), gcols)
        for i, ref in enumerate((q_ref, k_ref, v_ref)):
            send[g, :, i] = dot(perm[...], ref[:, cols]).astype(low).reshape(nn, bucket, gcols)
        each(nn, lambda d: in_copy(g, d, me).start())
        recv[g, me] = send[g, me]

    perm_send(0)
    if groups > 1:
        perm_send(1)

    each(nn, lambda d: g_copy(d, behind(d)).wait_recv())
    ga[...] = dot(grecv[:, :, :width].reshape(rows, width), w_ref[...]).astype(low)
    tag_rows = grecv[:, :, width:].reshape(rows, TAG_LANES)
    bias[...] = jnp.where(dot_lanes(tag_rows, tag_rows) > 0.5, 0.0, big_negative)

    def rep_sum(g):
        each(rr, lambda d: w_copy(g, d, rep_behind(d)).wait_recv())
        total = wsend[g, mr].astype(jnp.float32)
        for d in range(1, rr):
            total = total + wrecv[g, rep_behind(d)].astype(jnp.float32)
        nsend[g] = total.astype(low)
        each(nn, lambda d: n_copy(g, d, me).start())

    def node_sum(g):
        each(nn, lambda d: n_copy(g, d, behind(d)).wait_recv())
        total = nsend[g, me].astype(jnp.float32)
        for d in range(1, nn):
            total = total + nrecv[g, behind(d)].astype(jnp.float32)
        cols = pl.ds(pl.multiple_of(g * gcols, HEAD_DIM), gcols)
        fsend[:, cols] = total.astype(low)

    def put_back(g):
        each(nn, lambda d: back_copy(g, d, behind(d)).wait_recv())
        cols = pl.ds(pl.multiple_of(g * gcols, HEAD_DIM), gcols)
        for i, ref in enumerate((dq_ref, dk_ref, dv_ref)):
            ref[:, cols] = dot(unperm[...], brecv[g, :, i].reshape(rows, gcols)).astype(low)

    def group_step(g, carry):
        @pl.when(g + 2 < groups)
        def _():
            perm_send(g + 2)

        each(nn, lambda d: in_copy(g, d, behind(d)).wait_recv())
        for h in range(gcols // HEAD_DIM):
            hc = slice(h * HEAD_DIM, (h + 1) * HEAD_DIM)
            q = recv[g, :, 0, :, hc].reshape(rows, HEAD_DIM)
            k = recv[g, :, 1, :, hc].reshape(rows, HEAD_DIM)
            v = recv[g, :, 2, :, hc].reshape(rows, HEAD_DIM)
            gr = ga[:, pl.ds(pl.multiple_of(g * gcols + h * HEAD_DIM, HEAD_DIM), HEAD_DIM)]
            scores = dot_lanes(q, k) * scale + bias[...]
            weights = jnp.exp(scores - jnp.max(scores, axis=1, keepdims=True))
            probs = weights / jnp.sum(weights, axis=1, keepdims=True)
            probs_low = probs.astype(low)
            attended = dot(probs_low, v).astype(low)
            att[:, hc] = attended
            delta = jnp.sum(
                gr.astype(jnp.float32) * attended.astype(jnp.float32), axis=1, keepdims=True)
            ds = (probs * (dot_lanes(gr, v) - delta) * scale).astype(low)
            shape = (nn, bucket, HEAD_DIM)
            bsend[g, :, 0, :, hc] = dot(ds, k).astype(low).reshape(shape)
            bsend[g, :, 1, :, hc] = dot_rows(ds, q).astype(low).reshape(shape)
            bsend[g, :, 2, :, hc] = dot_rows(probs_low, gr).astype(low).reshape(shape)
        each(nn, lambda d: back_copy(g, d, me).start())
        brecv[g, me] = bsend[g, me]
        share = dot_rows(grecv[:, :, :width].reshape(rows, width), att[...]) * norm_factor
        share = share.astype(low).reshape(nn, rr, seg, gcols)
        for r in range(rr):
            wsend[g, r] = share[:, r]
        each(rr, lambda d: w_copy(g, d, mr).start())

        @pl.when(g >= 1)
        def _():
            rep_sum(g - 1)

        @pl.when(g >= 2)
        def _():
            node_sum(g - 2)

        return carry

    lax.fori_loop(0, groups, group_step, 0)
    rep_sum(groups - 1)

    def early(g, carry):
        put_back(g)
        return carry

    lax.fori_loop(0, groups - 1, early, 0)
    if groups > 1:
        node_sum(groups - 2)
    node_sum(groups - 1)
    each(rr, lambda d: f_copy(d, mr).start())
    put_back(groups - 1)
    frecv[mr] = fsend[...]
    each(rr, lambda d: f_copy(d, rep_behind(d)).wait_recv())
    dw_ref[...] = frecv[...].reshape(rr * seg, width).astype(jnp.float32)

    each(nn, lambda d: g_copy(d, me).wait_send())

    def drain(g, carry):
        each(nn, lambda d: in_copy(g, d, me).wait_send())
        each(nn, lambda d: back_copy(g, d, me).wait_send())
        each(nn, lambda d: n_copy(g, d, me).wait_send())
        each(rr, lambda d: w_copy(g, d, mr).wait_send())
        return carry

    lax.fori_loop(0, groups, drain, 0)
    each(rr, lambda d: f_copy(d, mr).wait_send())


def local_kernel(queries, keys, values, grad_out, w_out, cluster_id):
    nn = lax.axis_size("nodes")
    rr = lax.axis_size("rep")
    rows, width = queries.shape[1:]
    bucket = rows // nn
    groups = width // HEAD_DIM // GROUP_HEADS
    gcols = width // groups
    seg = width // (nn * rr)
    norm_factor = 1.0 / math.sqrt(rr * nn * rows)
    low = jnp.bfloat16
    ids = cluster_id[0]
    owners = ids // CL_DEV
    subs = ids - owners * CL_DEV
    table = owners[:, None] == jnp.arange(nn, dtype=jnp.int32)[None, :]
    number = jnp.arange(rows, dtype=jnp.int32)
    earlier = (number[:, None] > number[None, :]).astype(low)
    before = jnp.dot(earlier, table.astype(low), preferred_element_type=jnp.float32)
    rank = jnp.sum(jnp.where(table, before, 0.0), axis=1).astype(jnp.int32)
    slot = owners * bucket + rank
    tags = (subs[:, None] == jnp.arange(TAG_LANES, dtype=jnp.int32)[None, :]).astype(low)
    vmem = pl.BlockSpec(memory_space=pltpu.VMEM)
    dma = pltpu.SemaphoreType.DMA
    ext = width + TAG_LANES
    outs = pl.pallas_call(
        functools.partial(layer_kernel, nn, rr, groups, norm_factor),
        out_shape=[jax.ShapeDtypeStruct((rows, width), low)] * 3
        + [jax.ShapeDtypeStruct((rr * seg, width), jnp.float32)],
        in_specs=[vmem] * 8,
        out_specs=[vmem] * 4,
        scratch_shapes=[
            pltpu.VMEM((rows, rows), low),
            pltpu.VMEM((rows, rows), low),
            pltpu.VMEM((nn, bucket, ext), low),
            pltpu.VMEM((nn, bucket, ext), low),
            pltpu.VMEM((groups, nn, 3, bucket, gcols), low),
            pltpu.VMEM((groups, nn, 3, bucket, gcols), low),
            pltpu.VMEM((rows, width), low),
            pltpu.VMEM((rows, rows), jnp.float32),
            pltpu.VMEM((rows, gcols), low),
            pltpu.VMEM((groups, nn, 3, bucket, gcols), low),
            pltpu.VMEM((groups, nn, 3, bucket, gcols), low),
            pltpu.VMEM((groups, rr, nn, seg, gcols), low),
            pltpu.VMEM((groups, rr, nn, seg, gcols), low),
            pltpu.VMEM((groups, nn, seg, gcols), low),
            pltpu.VMEM((groups, nn, seg, gcols), low),
            pltpu.VMEM((seg, width), low),
            pltpu.VMEM((rr, seg, width), low),
            dma((nn,)), dma((nn,)),
            dma((groups, nn)), dma((groups, nn)),
            dma((groups, nn)), dma((groups, nn)),
            dma((groups, rr)), dma((groups, rr)),
            dma((groups, nn)), dma((groups, nn)),
            dma((rr,)), dma((rr,)),
        ],
        compiler_params=pltpu.CompilerParams(
            collective_id=0, has_side_effects=True, vmem_limit_bytes=56 * 1024 * 1024
        ),
    )(slot[None, :], slot[:, None], tags, queries[0], keys[0], values[0], grad_out[0], w_out)
    return (outs[0][None], outs[1][None], outs[2][None], outs[3])


def local(queries, keys, values, grad_out, w_out, cluster_id):
    nn, rr = lax.axis_size("nodes"), lax.axis_size("rep")
    rows, width = queries.shape[1:]
    heads = width // HEAD_DIM
    fits = (
        rows % (16 * nn) == 0 and width % (16 * nn * rr) == 0 and heads % GROUP_HEADS == 0
        and CL_DEV <= TAG_LANES and nn > 1 and rr > 1
    )
    chosen = local_kernel if fits else local_plain
    return chosen(queries, keys, values, grad_out, w_out, cluster_id)


def solution(mesh):
    in_specs = (
        P("rep", "nodes", None),
        P("rep", "nodes", None),
        P("rep", "nodes", None),
        P("rep", "nodes", None),
        P(),
        P("rep", "nodes"),
    )
    out_specs = (
        P("rep", "nodes", None),
        P("rep", "nodes", None),
        P("rep", "nodes", None),
        P("nodes", None),
    )
    return jax.shard_map(local, mesh=mesh, in_specs=in_specs, out_specs=out_specs, check_vma=False)
```

```python
import functools
import itertools
import math

import jax
import jax.numpy as jnp
from jax import lax
from jax.experimental import pallas as pl
from jax.experimental.pallas import tpu as pltpu
from jax.sharding import PartitionSpec as P

HEAD_DIM = 128
CL_DEV = 4
GROUP_HEADS = 4
TAG_ROWS = 16
TAG_LANES = 128
MESH = pl.DeviceIdType.MESH


big_negative = -1e30


def head_grads(query_rows, key_rows, value_rows, grad_rows, tag_rows, score_scale):
    scores = (
        lax.dot_general(
            query_rows, key_rows, (((1,), (1,)), ((), ())), preferred_element_type=jnp.float32
        )
        * score_scale
    )
    allowed = (tag_rows[:, None] == tag_rows[None, :]) & (tag_rows[None, :] > 0)
    scores = jnp.where(allowed, scores, big_negative)
    highest = jnp.max(scores, axis=1, keepdims=True)
    weights = jnp.exp(scores - highest)
    softmax_rows = weights / jnp.sum(weights, axis=1, keepdims=True)
    softmax_low = softmax_rows.astype(jnp.bfloat16)
    attended = jnp.dot(softmax_low, value_rows, preferred_element_type=jnp.float32).astype(
        jnp.bfloat16
    )
    delta_rows = jnp.sum(
        grad_rows.astype(jnp.float32) * attended.astype(jnp.float32), axis=1, keepdims=True
    )
    grad_softmax = lax.dot_general(
        grad_rows, value_rows, (((1,), (1,)), ((), ())), preferred_element_type=jnp.float32
    )
    grad_scores = (softmax_rows * (grad_softmax - delta_rows) * score_scale).astype(jnp.bfloat16)
    grad_query = jnp.dot(grad_scores, key_rows, preferred_element_type=jnp.float32).astype(
        jnp.bfloat16
    )
    grad_key = lax.dot_general(
        grad_scores, query_rows, (((0,), (0,)), ((), ())), preferred_element_type=jnp.float32
    ).astype(jnp.bfloat16)
    grad_value = lax.dot_general(
        softmax_low, grad_rows, (((0,), (0,)), ((), ())), preferred_element_type=jnp.float32
    ).astype(jnp.bfloat16)
    return (grad_query, grad_key, grad_value, attended)


def all_heads(query_all, key_all, value_all, grad_all, tag_all, score_scale):
    collected = [[], [], [], []]
    for head_index in range(query_all.shape[1]):
        outputs = head_grads(
            query_all[:, head_index],
            key_all[:, head_index],
            value_all[:, head_index],
            grad_all[:, head_index],
            tag_all[:, head_index],
            score_scale,
        )
        for member in range(4):
            collected[member].append(outputs[member])
    return tuple((jnp.stack(pieces_list, axis=1) for pieces_list in collected))


def local_plain(queries, keys, values, grad_out, w_out, cluster_id):
    node_count = lax.axis_size("nodes")
    rows_here = queries.shape[1]
    model_width = queries.shape[2]
    head_count = model_width // HEAD_DIM
    bucket = rows_here // node_count
    buffer_rows = node_count * bucket
    head_shape = (buffer_rows, head_count, HEAD_DIM)
    score_scale = 1.0 / math.sqrt(HEAD_DIM)
    norm_factor = 1.0 / math.sqrt(lax.axis_size("rep") * node_count * rows_here)
    cluster_ids = cluster_id[0]
    owner_ids = cluster_ids // CL_DEV
    sub_ids = cluster_ids - owner_ids * CL_DEV
    owner_table = (owner_ids[:, None] == jnp.arange(node_count, dtype=jnp.int32)[None, :]).astype(
        jnp.float32
    )
    row_numbers = jnp.arange(rows_here, dtype=jnp.int32)
    earlier = (row_numbers[:, None] > row_numbers[None, :]).astype(jnp.float32)
    before = jnp.dot(earlier, owner_table, precision=lax.Precision.HIGHEST)
    rank_in_bucket = jnp.sum(before * owner_table, axis=1).astype(jnp.int32)
    slot_index = owner_ids * bucket + rank_in_bucket

    def to_buffer(rows):
        return jnp.zeros((buffer_rows,) + rows.shape[1:], rows.dtype).at[slot_index].set(rows)

    tag_column = to_buffer((sub_ids + 1).astype(jnp.bfloat16))
    tag_grid = jnp.broadcast_to(tag_column[:, None], (buffer_rows, head_count))
    query_local = queries[0]
    key_local = keys[0]
    value_local = values[0]
    grad_local = grad_out[0]
    arrived = (
        lax.all_to_all(to_buffer(query_local), "nodes", split_axis=0, concat_axis=0, tiled=True),
        lax.all_to_all(to_buffer(key_local), "nodes", split_axis=0, concat_axis=0, tiled=True),
        lax.all_to_all(to_buffer(value_local), "nodes", split_axis=0, concat_axis=0, tiled=True),
        lax.all_to_all(to_buffer(grad_local), "nodes", split_axis=0, concat_axis=0, tiled=True),
        lax.all_to_all(tag_grid, "nodes", split_axis=0, concat_axis=0, tiled=True),
    )
    query_recv, key_recv, value_recv, grad_recv, tag_recv = arrived
    grad_attended = jnp.dot(grad_recv, w_out, preferred_element_type=jnp.float32).astype(
        jnp.bfloat16
    )
    results = all_heads(
        query_recv.reshape(head_shape),
        key_recv.reshape(head_shape),
        value_recv.reshape(head_shape),
        grad_attended.reshape(head_shape),
        tag_recv,
        score_scale,
    )
    flattened = [result.reshape(buffer_rows, model_width) for result in results]
    returned = (
        lax.all_to_all(flattened[0], "nodes", split_axis=0, concat_axis=0, tiled=True),
        lax.all_to_all(flattened[1], "nodes", split_axis=0, concat_axis=0, tiled=True),
        lax.all_to_all(flattened[2], "nodes", split_axis=0, concat_axis=0, tiled=True),
    )
    grad_query = returned[0][slot_index]
    grad_key = returned[1][slot_index]
    grad_value = returned[2][slot_index]
    attended_rows = flattened[3]
    row_share = lax.psum_scatter(
        lax.dot_general(
            grad_recv, attended_rows, (((0,), (0,)), ((), ())), preferred_element_type=jnp.float32
        )
        * norm_factor,
        "nodes",
        scatter_dimension=0,
        tiled=True,
    )
    grad_weight = lax.psum(row_share.astype(jnp.bfloat16), "rep").astype(jnp.float32)
    return (grad_query[None], grad_key[None], grad_value[None], grad_weight)


def dot_rows(a, b):
    return lax.dot_general(a, b, (((0,), (0,)), ((), ())), preferred_element_type=jnp.float32)


def dot_lanes(a, b):
    return lax.dot_general(a, b, (((1,), (1,)), ((), ())), preferred_element_type=jnp.float32)


def dot(a, b):
    return jnp.dot(a, b, preferred_element_type=jnp.float32)


def layer_kernel(
    nn, rr, groups, norm_factor,
    ids_ref, q_ref, k_ref, v_ref, g_ref, w_ref,
    dq_ref, dk_ref, dv_ref, dw_ref,
    perm, unperm, gsend, grecv, tsend, trecv, send, recv, ga, bias, att, bsend, brecv,
    wsend, wrecv, nsend, nrecv, fsend, frecv,
    g_ss, g_rs, t_ss, t_rs, in_ss, in_rs, b_ss, b_rs, w_ss, w_rs, n_ss, n_rs, f_ss, f_rs,
):
    low = jnp.bfloat16
    me = lax.axis_index("nodes")
    mr = lax.axis_index("rep")
    rows, width = q_ref.shape
    bucket = rows // nn
    gcols = width // groups
    seg = width // (nn * rr)
    scale = 1.0 / math.sqrt(HEAD_DIM)

    paired = nn & (nn - 1) == 0
    near, far = list(range(1, nn // 2)), list(range(max(nn // 2, 1), nn))
    order = [d for two in itertools.zip_longest(far, near) for d in two if d is not None]

    def flipped(d):
        peer, bit = me, 1
        while bit < nn:
            if d & bit:
                peer = peer + bit - 2 * bit * lax.rem(me // bit, 2)
            bit *= 2
        return peer

    def ahead(d):
        return flipped(d) if paired else lax.rem(me + d, nn)

    def behind(d):
        return flipped(d) if paired else lax.rem(me + nn - d, nn)

    def rep_ahead(d):
        return lax.rem(mr + d, rr)

    def rep_behind(d):
        return lax.rem(mr + rr - d, rr)

    def g_copy(d, slot):
        peer = ahead(d)
        return pltpu.make_async_remote_copy(
            src_ref=gsend.at[peer], dst_ref=grecv.at[slot], send_sem=g_ss.at[d],
            recv_sem=g_rs.at[d], device_id={"nodes": peer}, device_id_type=MESH)

    def t_copy(d, slot):
        peer = ahead(d)
        return pltpu.make_async_remote_copy(
            src_ref=tsend.at[peer], dst_ref=trecv.at[slot], send_sem=t_ss.at[d],
            recv_sem=t_rs.at[d], device_id={"nodes": peer}, device_id_type=MESH)

    def in_copy(g, d, slot):
        peer = ahead(d)
        return pltpu.make_async_remote_copy(
            src_ref=send.at[g, peer], dst_ref=recv.at[g, slot], send_sem=in_ss.at[g, d],
            recv_sem=in_rs.at[g, d], device_id={"nodes": peer}, device_id_type=MESH)

    def back_copy(g, d, slot):
        peer = ahead(d)
        return pltpu.make_async_remote_copy(
            src_ref=bsend.at[g, peer], dst_ref=brecv.at[g, slot], send_sem=b_ss.at[g, d],
            recv_sem=b_rs.at[g, d], device_id={"nodes": peer}, device_id_type=MESH)

    def w_copy(g, d, slot):
        peer = rep_ahead(d)
        return pltpu.make_async_remote_copy(
            src_ref=wsend.at[g, peer], dst_ref=wrecv.at[g, slot], send_sem=w_ss.at[g, d],
            recv_sem=w_rs.at[g, d], device_id={"rep": peer}, device_id_type=MESH)

    def n_copy(g, d, slot):
        peer = ahead(d)
        return pltpu.make_async_remote_copy(
            src_ref=nsend.at[g, peer], dst_ref=nrecv.at[g, slot], send_sem=n_ss.at[g, d],
            recv_sem=n_rs.at[g, d], device_id={"nodes": peer}, device_id_type=MESH)

    def f_copy(d, slot):
        peer = rep_ahead(d)
        return pltpu.make_async_remote_copy(
            src_ref=fsend, dst_ref=frecv.at[slot], send_sem=f_ss.at[d],
            recv_sem=f_rs.at[d], device_id={"rep": peer}, device_id_type=MESH)

    def each(count, act):
        def step(d, carry):
            act(d)
            return carry

        lax.fori_loop(1, count, step, 0)

    def peers(act):
        for d in order:
            act(d)

    barrier = pltpu.get_barrier_semaphore()
    for d in range(1, nn):
        pl.semaphore_signal(barrier, inc=1, device_id={"nodes": ahead(d)}, device_id_type=MESH)
    for d in range(1, rr):
        pl.semaphore_signal(barrier, inc=1, device_id={"rep": rep_ahead(d)}, device_id_type=MESH)

    ids = ids_ref[...]
    owners = ids // CL_DEV
    owner_table = jnp.where(
        lax.broadcasted_iota(jnp.int32, (max(nn, 8), rows), 0) == owners, 1.0, 0.0)
    tag_table = jnp.where(
        lax.broadcasted_iota(jnp.int32, (TAG_ROWS, rows), 0) == ids - owners * CL_DEV, 1.0, 0.0)
    down = lax.broadcasted_iota(jnp.int32, (rows, rows), 0)
    across = lax.broadcasted_iota(jnp.int32, (rows, rows), 1)
    before = dot(owner_table.astype(low), jnp.where(down < across, 1.0, 0.0).astype(low))
    rank = jnp.sum(before * owner_table, axis=0, keepdims=True).astype(jnp.int32)
    perm_wide = jnp.where(down == owners * bucket + rank, 1.0, 0.0)
    perm[...] = perm_wide.astype(low)
    gsend[...] = dot(perm[...], g_ref[...]).astype(low).reshape(nn, bucket, width)
    pl.semaphore_wait(barrier, nn + rr - 2)
    peers(lambda d: g_copy(d, me).start())
    grecv[me] = gsend[me]
    tag_line = dot_lanes(tag_table.astype(low), perm[...]).astype(low)
    tall = lax.broadcasted_iota(jnp.int32, (rows, TAG_LANES), 0)
    lane = lax.broadcasted_iota(jnp.int32, (rows, TAG_LANES), 1)
    for o in range(nn):
        pick = jnp.where((tall - lane == o * bucket) & (lane < bucket), 1.0, 0.0).astype(low)
        tsend[o] = dot(tag_line, pick).astype(low)
    peers(lambda d: t_copy(d, me).start())
    trecv[me] = tsend[me]

    def perm_send(g):
        cols = pl.ds(pl.multiple_of(g * gcols, HEAD_DIM), gcols)
        for i, ref in enumerate((q_ref, k_ref, v_ref)):
            send[g, :, i] = dot(perm[...], ref[:, cols]).astype(low).reshape(nn, bucket, gcols)
        peers(lambda d: in_copy(g, d, me).start())
        recv[g, me] = send[g, me]

    perm_send(0)
    if groups > 1:
        perm_send(1)
    unperm[...] = jnp.transpose(perm_wide).astype(low)
    peers(lambda d: t_copy(d, behind(d)).wait_recv())
    tag_all = jnp.zeros((TAG_ROWS, rows), jnp.float32)
    high = lax.broadcasted_iota(jnp.int32, (TAG_LANES, rows), 0)
    wide = lax.broadcasted_iota(jnp.int32, (TAG_LANES, rows), 1)
    for o in range(nn):
        place = jnp.where(wide - high == o * bucket, 1.0, 0.0).astype(low)
        tag_all = tag_all + dot(trecv[o], place)
    tag_all = tag_all.astype(low)
    bias[...] = jnp.where(dot_rows(tag_all, tag_all) > 0.5, 0.0, big_negative)

    peers(lambda d: g_copy(d, behind(d)).wait_recv())
    ga[...] = dot(grecv[...].reshape(rows, width), w_ref[...]).astype(low)

    def rep_sum(g):
        each(rr, lambda d: w_copy(g, d, rep_behind(d)).wait_recv())
        total = wsend[g, mr].astype(jnp.float32)
        for d in range(1, rr):
            total = total + wrecv[g, rep_behind(d)].astype(jnp.float32)
        nsend[g] = total.astype(low)
        peers(lambda d: n_copy(g, d, me).start())

    def node_sum(g):
        peers(lambda d: n_copy(g, d, behind(d)).wait_recv())
        total = nsend[g, me].astype(jnp.float32)
        for d in range(1, nn):
            total = total + nrecv[g, behind(d)].astype(jnp.float32)
        cols = pl.ds(pl.multiple_of(g * gcols, HEAD_DIM), gcols)
        fsend[:, cols] = total.astype(low)

    def put_back(g):
        peers(lambda d: back_copy(g, d, behind(d)).wait_recv())
        cols = pl.ds(pl.multiple_of(g * gcols, HEAD_DIM), gcols)
        for i, ref in enumerate((dq_ref, dk_ref, dv_ref)):
            ref[:, cols] = dot(unperm[...], brecv[g, :, i].reshape(rows, gcols)).astype(low)

    def group_step(g, carry):
        @pl.when(g + 2 < groups)
        def _():
            perm_send(g + 2)

        peers(lambda d: in_copy(g, d, behind(d)).wait_recv())
        for h in range(gcols // HEAD_DIM):
            hc = slice(h * HEAD_DIM, (h + 1) * HEAD_DIM)
            q = recv[g, :, 0, :, hc].reshape(rows, HEAD_DIM)
            k = recv[g, :, 1, :, hc].reshape(rows, HEAD_DIM)
            v = recv[g, :, 2, :, hc].reshape(rows, HEAD_DIM)
            gr = ga[:, pl.ds(pl.multiple_of(g * gcols + h * HEAD_DIM, HEAD_DIM), HEAD_DIM)]
            scores = dot_lanes(q, k) * scale + bias[...]
            weights = jnp.exp(scores - jnp.max(scores, axis=1, keepdims=True))
            probs = weights / jnp.sum(weights, axis=1, keepdims=True)
            probs_low = probs.astype(low)
            attended = dot(probs_low, v).astype(low)
            att[:, hc] = attended
            delta = jnp.sum(
                gr.astype(jnp.float32) * attended.astype(jnp.float32), axis=1, keepdims=True)
            ds = (probs * (dot_lanes(gr, v) - delta) * scale).astype(low)
            shape = (nn, bucket, HEAD_DIM)
            bsend[g, :, 0, :, hc] = dot(ds, k).astype(low).reshape(shape)
            bsend[g, :, 1, :, hc] = dot_rows(ds, q).astype(low).reshape(shape)
            bsend[g, :, 2, :, hc] = dot_rows(probs_low, gr).astype(low).reshape(shape)
        peers(lambda d: back_copy(g, d, me).start())
        brecv[g, me] = bsend[g, me]
        share = dot_rows(grecv[...].reshape(rows, width), att[...]) * norm_factor
        share = share.astype(low).reshape(nn, rr, seg, gcols)
        for r in range(rr):
            wsend[g, r] = share[:, r]
        each(rr, lambda d: w_copy(g, d, mr).start())

        @pl.when(g >= 1)
        def _():
            rep_sum(g - 1)

        @pl.when(g >= 2)
        def _():
            node_sum(g - 2)

        return carry

    lax.fori_loop(0, groups, group_step, 0)
    rep_sum(groups - 1)

    def early(g, carry):
        put_back(g)
        return carry

    lax.fori_loop(0, groups - 1, early, 0)
    if groups > 1:
        node_sum(groups - 2)
    node_sum(groups - 1)
    each(rr, lambda d: f_copy(d, mr).start())
    put_back(groups - 1)
    frecv[mr] = fsend[...]
    each(rr, lambda d: f_copy(d, rep_behind(d)).wait_recv())
    dw_ref[...] = frecv[...].reshape(rr * seg, width)

    peers(lambda d: g_copy(d, me).wait_send())
    peers(lambda d: t_copy(d, me).wait_send())

    def drain(g, carry):
        peers(lambda d: in_copy(g, d, me).wait_send())
        peers(lambda d: back_copy(g, d, me).wait_send())
        peers(lambda d: n_copy(g, d, me).wait_send())
        each(rr, lambda d: w_copy(g, d, mr).wait_send())
        return carry

    lax.fori_loop(0, groups, drain, 0)
    each(rr, lambda d: f_copy(d, mr).wait_send())


def local_kernel(queries, keys, values, grad_out, w_out, cluster_id):
    nn = lax.axis_size("nodes")
    rr = lax.axis_size("rep")
    rows, width = queries.shape[1:]
    bucket = rows // nn
    groups = width // HEAD_DIM // GROUP_HEADS
    gcols = width // groups
    seg = width // (nn * rr)
    norm_factor = 1.0 / math.sqrt(rr * nn * rows)
    low = jnp.bfloat16
    vmem = pl.BlockSpec(memory_space=pltpu.VMEM)
    dma = pltpu.SemaphoreType.DMA
    outs = pl.pallas_call(
        functools.partial(layer_kernel, nn, rr, groups, norm_factor),
        out_shape=[jax.ShapeDtypeStruct((rows, width), low)] * 3
        + [jax.ShapeDtypeStruct((rr * seg, width), low)],
        in_specs=[vmem] * 6,
        out_specs=[vmem] * 4,
        scratch_shapes=[
            pltpu.VMEM((rows, rows), low),
            pltpu.VMEM((rows, rows), low),
            pltpu.VMEM((nn, bucket, width), low),
            pltpu.VMEM((nn, bucket, width), low),
            pltpu.VMEM((nn, TAG_ROWS, TAG_LANES), low),
            pltpu.VMEM((nn, TAG_ROWS, TAG_LANES), low),
            pltpu.VMEM((groups, nn, 3, bucket, gcols), low),
            pltpu.VMEM((groups, nn, 3, bucket, gcols), low),
            pltpu.VMEM((rows, width), low),
            pltpu.VMEM((rows, rows), jnp.float32),
            pltpu.VMEM((rows, gcols), low),
            pltpu.VMEM((groups, nn, 3, bucket, gcols), low),
            pltpu.VMEM((groups, nn, 3, bucket, gcols), low),
            pltpu.VMEM((groups, rr, nn, seg, gcols), low),
            pltpu.VMEM((groups, rr, nn, seg, gcols), low),
            pltpu.VMEM((groups, nn, seg, gcols), low),
            pltpu.VMEM((groups, nn, seg, gcols), low),
            pltpu.VMEM((seg, width), low),
            pltpu.VMEM((rr, seg, width), low),
            dma((nn,)), dma((nn,)),
            dma((nn,)), dma((nn,)),
            dma((groups, nn)), dma((groups, nn)),
            dma((groups, nn)), dma((groups, nn)),
            dma((groups, rr)), dma((groups, rr)),
            dma((groups, nn)), dma((groups, nn)),
            dma((rr,)), dma((rr,)),
        ],
        compiler_params=pltpu.CompilerParams(
            collective_id=0, has_side_effects=True, vmem_limit_bytes=56 * 1024 * 1024
        ),
    )(cluster_id, queries[0], keys[0], values[0], grad_out[0], w_out)
    return (outs[0][None], outs[1][None], outs[2][None], outs[3].astype(jnp.float32))


def local(queries, keys, values, grad_out, w_out, cluster_id):
    nn, rr = lax.axis_size("nodes"), lax.axis_size("rep")
    rows, width = queries.shape[1:]
    heads = width // HEAD_DIM
    bucket_fits = rows // nn <= TAG_LANES
    fits = (
        rows % (16 * nn) == 0 and width % (16 * nn * rr) == 0 and heads % GROUP_HEADS == 0
        and CL_DEV <= TAG_ROWS and bucket_fits and nn > 1 and rr > 1
    )
    chosen = local_kernel if fits else local_plain
    return chosen(queries, keys, values, grad_out, w_out, cluster_id)


def solution(mesh):
    in_specs = (
        P("rep", "nodes", None),
        P("rep", "nodes", None),
        P("rep", "nodes", None),
        P("rep", "nodes", None),
        P(),
        P("rep", "nodes"),
    )
    out_specs = (
        P("rep", "nodes", None),
        P("rep", "nodes", None),
        P("rep", "nodes", None),
        P("nodes", None),
    )
    return jax.shard_map(local, mesh=mesh, in_specs=in_specs, out_specs=out_specs, check_vma=False)
```

```python
import functools
import itertools
import math

import jax
import jax.numpy as jnp
from jax import lax
from jax.experimental import pallas as pl
from jax.experimental.pallas import tpu as pltpu
from jax.sharding import PartitionSpec as P

HEAD_DIM = 128
CL_DEV = 4
GROUP_HEADS = 4
TAG_ROWS = 16
TAG_LANES = 128
MESH = pl.DeviceIdType.MESH


big_negative = -1e30


def head_grads(query_rows, key_rows, value_rows, grad_rows, tag_rows, score_scale):
    scores = (
        lax.dot_general(
            query_rows, key_rows, (((1,), (1,)), ((), ())), preferred_element_type=jnp.float32
        )
        * score_scale
    )
    allowed = (tag_rows[:, None] == tag_rows[None, :]) & (tag_rows[None, :] > 0)
    scores = jnp.where(allowed, scores, big_negative)
    highest = jnp.max(scores, axis=1, keepdims=True)
    weights = jnp.exp(scores - highest)
    softmax_rows = weights / jnp.sum(weights, axis=1, keepdims=True)
    softmax_low = softmax_rows.astype(jnp.bfloat16)
    attended = jnp.dot(softmax_low, value_rows, preferred_element_type=jnp.float32).astype(
        jnp.bfloat16
    )
    delta_rows = jnp.sum(
        grad_rows.astype(jnp.float32) * attended.astype(jnp.float32), axis=1, keepdims=True
    )
    grad_softmax = lax.dot_general(
        grad_rows, value_rows, (((1,), (1,)), ((), ())), preferred_element_type=jnp.float32
    )
    grad_scores = (softmax_rows * (grad_softmax - delta_rows) * score_scale).astype(jnp.bfloat16)
    grad_query = jnp.dot(grad_scores, key_rows, preferred_element_type=jnp.float32).astype(
        jnp.bfloat16
    )
    grad_key = lax.dot_general(
        grad_scores, query_rows, (((0,), (0,)), ((), ())), preferred_element_type=jnp.float32
    ).astype(jnp.bfloat16)
    grad_value = lax.dot_general(
        softmax_low, grad_rows, (((0,), (0,)), ((), ())), preferred_element_type=jnp.float32
    ).astype(jnp.bfloat16)
    return (grad_query, grad_key, grad_value, attended)


def all_heads(query_all, key_all, value_all, grad_all, tag_all, score_scale):
    collected = [[], [], [], []]
    for head_index in range(query_all.shape[1]):
        outputs = head_grads(
            query_all[:, head_index],
            key_all[:, head_index],
            value_all[:, head_index],
            grad_all[:, head_index],
            tag_all[:, head_index],
            score_scale,
        )
        for member in range(4):
            collected[member].append(outputs[member])
    return tuple((jnp.stack(pieces_list, axis=1) for pieces_list in collected))


def local_plain(queries, keys, values, grad_out, w_out, cluster_id):
    node_count = lax.axis_size("nodes")
    rows_here = queries.shape[1]
    model_width = queries.shape[2]
    head_count = model_width // HEAD_DIM
    bucket = rows_here // node_count
    buffer_rows = node_count * bucket
    head_shape = (buffer_rows, head_count, HEAD_DIM)
    score_scale = 1.0 / math.sqrt(HEAD_DIM)
    norm_factor = 1.0 / math.sqrt(lax.axis_size("rep") * node_count * rows_here)
    cluster_ids = cluster_id[0]
    owner_ids = cluster_ids // CL_DEV
    sub_ids = cluster_ids - owner_ids * CL_DEV
    owner_table = (owner_ids[:, None] == jnp.arange(node_count, dtype=jnp.int32)[None, :]).astype(
        jnp.float32
    )
    row_numbers = jnp.arange(rows_here, dtype=jnp.int32)
    earlier = (row_numbers[:, None] > row_numbers[None, :]).astype(jnp.float32)
    before = jnp.dot(earlier, owner_table, precision=lax.Precision.HIGHEST)
    rank_in_bucket = jnp.sum(before * owner_table, axis=1).astype(jnp.int32)
    slot_index = owner_ids * bucket + rank_in_bucket

    def to_buffer(rows):
        return jnp.zeros((buffer_rows,) + rows.shape[1:], rows.dtype).at[slot_index].set(rows)

    tag_column = to_buffer((sub_ids + 1).astype(jnp.bfloat16))
    tag_grid = jnp.broadcast_to(tag_column[:, None], (buffer_rows, head_count))
    query_local = queries[0]
    key_local = keys[0]
    value_local = values[0]
    grad_local = grad_out[0]
    arrived = (
        lax.all_to_all(to_buffer(query_local), "nodes", split_axis=0, concat_axis=0, tiled=True),
        lax.all_to_all(to_buffer(key_local), "nodes", split_axis=0, concat_axis=0, tiled=True),
        lax.all_to_all(to_buffer(value_local), "nodes", split_axis=0, concat_axis=0, tiled=True),
        lax.all_to_all(to_buffer(grad_local), "nodes", split_axis=0, concat_axis=0, tiled=True),
        lax.all_to_all(tag_grid, "nodes", split_axis=0, concat_axis=0, tiled=True),
    )
    query_recv, key_recv, value_recv, grad_recv, tag_recv = arrived
    grad_attended = jnp.dot(grad_recv, w_out, preferred_element_type=jnp.float32).astype(
        jnp.bfloat16
    )
    results = all_heads(
        query_recv.reshape(head_shape),
        key_recv.reshape(head_shape),
        value_recv.reshape(head_shape),
        grad_attended.reshape(head_shape),
        tag_recv,
        score_scale,
    )
    flattened = [result.reshape(buffer_rows, model_width) for result in results]
    returned = (
        lax.all_to_all(flattened[0], "nodes", split_axis=0, concat_axis=0, tiled=True),
        lax.all_to_all(flattened[1], "nodes", split_axis=0, concat_axis=0, tiled=True),
        lax.all_to_all(flattened[2], "nodes", split_axis=0, concat_axis=0, tiled=True),
    )
    grad_query = returned[0][slot_index]
    grad_key = returned[1][slot_index]
    grad_value = returned[2][slot_index]
    attended_rows = flattened[3]
    row_share = lax.psum_scatter(
        lax.dot_general(
            grad_recv, attended_rows, (((0,), (0,)), ((), ())), preferred_element_type=jnp.float32
        )
        * norm_factor,
        "nodes",
        scatter_dimension=0,
        tiled=True,
    )
    grad_weight = lax.psum(row_share.astype(jnp.bfloat16), "rep").astype(jnp.float32)
    return (grad_query[None], grad_key[None], grad_value[None], grad_weight)


def dot_rows(a, b):
    return lax.dot_general(a, b, (((0,), (0,)), ((), ())), preferred_element_type=jnp.float32)


def dot_lanes(a, b):
    return lax.dot_general(a, b, (((1,), (1,)), ((), ())), preferred_element_type=jnp.float32)


def dot(a, b):
    return jnp.dot(a, b, preferred_element_type=jnp.float32)


def layer_kernel(
    nn, rr, groups, norm_factor,
    ids_ref, q_any, k_any, v_any, g_any, w_any,
    dq_ref, dk_ref, dv_ref, dw_ref,
    q_ref, k_ref, v_ref, g_ref, w_ref, load_sem, perm, unperm, gsend, grecv, tsend, trecv, send, recv, ga, bias, att, bsend, brecv,
    wsend, wrecv, nsend, nrecv, fsend, frecv,
    g_ss, g_rs, t_ss, t_rs, in_ss, in_rs, b_ss, b_rs, w_ss, w_rs, n_ss, n_rs, f_ss, f_rs,
):
    low = jnp.bfloat16
    me = lax.axis_index("nodes")
    mr = lax.axis_index("rep")
    rows, width = q_ref.shape
    bucket = rows // nn
    gcols = width // groups
    seg = width // (nn * rr)
    scale = 1.0 / math.sqrt(HEAD_DIM)

    paired = nn & (nn - 1) == 0
    near, far = list(range(1, nn // 2)), list(range(max(nn // 2, 1), nn))
    order = [d for two in itertools.zip_longest(far, near) for d in two if d is not None]

    def flipped(d):
        peer, bit = me, 1
        while bit < nn:
            if d & bit:
                peer = peer + bit - 2 * bit * lax.rem(me // bit, 2)
            bit *= 2
        return peer

    def ahead(d):
        return flipped(d) if paired else lax.rem(me + d, nn)

    def behind(d):
        return flipped(d) if paired else lax.rem(me + nn - d, nn)

    def rep_ahead(d):
        return lax.rem(mr + d, rr)

    def rep_behind(d):
        return lax.rem(mr + rr - d, rr)

    def g_copy(d, slot):
        peer = ahead(d)
        return pltpu.make_async_remote_copy(
            src_ref=gsend.at[peer], dst_ref=grecv.at[slot], send_sem=g_ss.at[d],
            recv_sem=g_rs.at[d], device_id={"nodes": peer}, device_id_type=MESH)

    def t_copy(d, slot):
        peer = ahead(d)
        return pltpu.make_async_remote_copy(
            src_ref=tsend.at[peer], dst_ref=trecv.at[slot], send_sem=t_ss.at[d],
            recv_sem=t_rs.at[d], device_id={"nodes": peer}, device_id_type=MESH)

    def in_copy(g, d, slot):
        peer = ahead(d)
        return pltpu.make_async_remote_copy(
            src_ref=send.at[g, peer], dst_ref=recv.at[g, slot], send_sem=in_ss.at[g, d],
            recv_sem=in_rs.at[g, d], device_id={"nodes": peer}, device_id_type=MESH)

    def back_copy(g, d, slot):
        peer = ahead(d)
        return pltpu.make_async_remote_copy(
            src_ref=bsend.at[g, peer], dst_ref=brecv.at[g, slot], send_sem=b_ss.at[g, d],
            recv_sem=b_rs.at[g, d], device_id={"nodes": peer}, device_id_type=MESH)

    def w_copy(g, d, slot):
        peer = rep_ahead(d)
        return pltpu.make_async_remote_copy(
            src_ref=wsend.at[g, peer], dst_ref=wrecv.at[g, slot], send_sem=w_ss.at[g, d],
            recv_sem=w_rs.at[g, d], device_id={"rep": peer}, device_id_type=MESH)

    def n_copy(g, d, slot):
        peer = ahead(d)
        return pltpu.make_async_remote_copy(
            src_ref=nsend.at[g, peer], dst_ref=nrecv.at[g, slot], send_sem=n_ss.at[g, d],
            recv_sem=n_rs.at[g, d], device_id={"nodes": peer}, device_id_type=MESH)

    def f_copy(d, slot):
        peer = rep_ahead(d)
        return pltpu.make_async_remote_copy(
            src_ref=fsend, dst_ref=frecv.at[slot], send_sem=f_ss.at[d],
            recv_sem=f_rs.at[d], device_id={"rep": peer}, device_id_type=MESH)

    def each(count, act):
        def step(d, carry):
            act(d)
            return carry

        lax.fori_loop(1, count, step, 0)

    def peers(act):
        for d in order:
            act(d)

    barrier = pltpu.get_barrier_semaphore()
    for d in range(1, nn):
        pl.semaphore_signal(barrier, inc=1, device_id={"nodes": ahead(d)}, device_id_type=MESH)
    for d in range(1, rr):
        pl.semaphore_signal(barrier, inc=1, device_id={"rep": rep_ahead(d)}, device_id_type=MESH)

    loads = [
        pltpu.make_async_copy(src, dst, load_sem.at[i])
        for i, (src, dst) in enumerate((
            (g_any, g_ref), (q_any, q_ref), (k_any, k_ref), (v_any, v_ref), (w_any, w_ref)))
    ]
    for load in loads:
        load.start()

    ids = ids_ref[...]
    owners = ids // CL_DEV
    owner_table = jnp.where(
        lax.broadcasted_iota(jnp.int32, (max(nn, 8), rows), 0) == owners, 1.0, 0.0)
    tag_table = jnp.where(
        lax.broadcasted_iota(jnp.int32, (TAG_ROWS, rows), 0) == ids - owners * CL_DEV, 1.0, 0.0)
    down = lax.broadcasted_iota(jnp.int32, (rows, rows), 0)
    across = lax.broadcasted_iota(jnp.int32, (rows, rows), 1)
    before = dot(owner_table.astype(low), jnp.where(down < across, 1.0, 0.0).astype(low))
    rank = jnp.sum(before * owner_table, axis=0, keepdims=True).astype(jnp.int32)
    perm_wide = jnp.where(down == owners * bucket + rank, 1.0, 0.0)
    perm[...] = perm_wide.astype(low)
    loads[0].wait()
    gsend[...] = dot(perm[...], g_ref[...]).astype(low).reshape(nn, bucket, width)
    pl.semaphore_wait(barrier, nn + rr - 2)
    peers(lambda d: g_copy(d, me).start())
    grecv[me] = gsend[me]
    tag_line = dot_lanes(tag_table.astype(low), perm[...]).astype(low)
    tall = lax.broadcasted_iota(jnp.int32, (rows, TAG_LANES), 0)
    lane = lax.broadcasted_iota(jnp.int32, (rows, TAG_LANES), 1)
    for o in range(nn):
        pick = jnp.where((tall - lane == o * bucket) & (lane < bucket), 1.0, 0.0).astype(low)
        tsend[o] = dot(tag_line, pick).astype(low)
    peers(lambda d: t_copy(d, me).start())
    trecv[me] = tsend[me]

    def perm_send(g):
        cols = pl.ds(pl.multiple_of(g * gcols, HEAD_DIM), gcols)
        for i, ref in enumerate((q_ref, k_ref, v_ref)):
            send[g, :, i] = dot(perm[...], ref[:, cols]).astype(low).reshape(nn, bucket, gcols)
        peers(lambda d: in_copy(g, d, me).start())
        recv[g, me] = send[g, me]

    for load in loads[1:]:
        load.wait()
    perm_send(0)
    if groups > 1:
        perm_send(1)
    unperm[...] = jnp.transpose(perm_wide).astype(low)
    peers(lambda d: t_copy(d, behind(d)).wait_recv())
    tag_all = jnp.zeros((TAG_ROWS, rows), jnp.float32)
    high = lax.broadcasted_iota(jnp.int32, (TAG_LANES, rows), 0)
    wide = lax.broadcasted_iota(jnp.int32, (TAG_LANES, rows), 1)
    for o in range(nn):
        place = jnp.where(wide - high == o * bucket, 1.0, 0.0).astype(low)
        tag_all = tag_all + dot(trecv[o], place)
    tag_all = tag_all.astype(low)
    bias[...] = jnp.where(dot_rows(tag_all, tag_all) > 0.5, 0.0, big_negative)

    peers(lambda d: g_copy(d, behind(d)).wait_recv())
    ga[...] = dot(grecv[...].reshape(rows, width), w_ref[...]).astype(low)

    def rep_sum(g):
        each(rr, lambda d: w_copy(g, d, rep_behind(d)).wait_recv())
        total = wsend[g, mr].astype(jnp.float32)
        for d in range(1, rr):
            total = total + wrecv[g, rep_behind(d)].astype(jnp.float32)
        nsend[g] = total.astype(low)
        peers(lambda d: n_copy(g, d, me).start())

    def node_sum(g):
        peers(lambda d: n_copy(g, d, behind(d)).wait_recv())
        total = nsend[g, me].astype(jnp.float32)
        for d in range(1, nn):
            total = total + nrecv[g, behind(d)].astype(jnp.float32)
        cols = pl.ds(pl.multiple_of(g * gcols, HEAD_DIM), gcols)
        fsend[:, cols] = total.astype(low)

    def put_back(g):
        peers(lambda d: back_copy(g, d, behind(d)).wait_recv())
        cols = pl.ds(pl.multiple_of(g * gcols, HEAD_DIM), gcols)
        for i, ref in enumerate((dq_ref, dk_ref, dv_ref)):
            ref[:, cols] = dot(unperm[...], brecv[g, :, i].reshape(rows, gcols)).astype(low)

    def group_step(g, carry):
        @pl.when(g + 2 < groups)
        def _():
            perm_send(g + 2)

        peers(lambda d: in_copy(g, d, behind(d)).wait_recv())
        for h in range(gcols // HEAD_DIM):
            hc = slice(h * HEAD_DIM, (h + 1) * HEAD_DIM)
            q = recv[g, :, 0, :, hc].reshape(rows, HEAD_DIM)
            k = recv[g, :, 1, :, hc].reshape(rows, HEAD_DIM)
            v = recv[g, :, 2, :, hc].reshape(rows, HEAD_DIM)
            gr = ga[:, pl.ds(pl.multiple_of(g * gcols + h * HEAD_DIM, HEAD_DIM), HEAD_DIM)]
            scores = dot_lanes(q, k) * scale + bias[...]
            weights = jnp.exp(scores - jnp.max(scores, axis=1, keepdims=True))
            probs = weights / jnp.sum(weights, axis=1, keepdims=True)
            probs_low = probs.astype(low)
            attended = dot(probs_low, v).astype(low)
            att[:, hc] = attended
            delta = jnp.sum(
                gr.astype(jnp.float32) * attended.astype(jnp.float32), axis=1, keepdims=True)
            ds = (probs * (dot_lanes(gr, v) - delta) * scale).astype(low)
            shape = (nn, bucket, HEAD_DIM)
            bsend[g, :, 0, :, hc] = dot(ds, k).astype(low).reshape(shape)
            bsend[g, :, 1, :, hc] = dot_rows(ds, q).astype(low).reshape(shape)
            bsend[g, :, 2, :, hc] = dot_rows(probs_low, gr).astype(low).reshape(shape)
        peers(lambda d: back_copy(g, d, me).start())
        brecv[g, me] = bsend[g, me]
        share = dot_rows(grecv[...].reshape(rows, width), att[...]) * norm_factor
        share = share.astype(low).reshape(nn, rr, seg, gcols)
        for r in range(rr):
            wsend[g, r] = share[:, r]
        each(rr, lambda d: w_copy(g, d, mr).start())

        @pl.when(g >= 1)
        def _():
            rep_sum(g - 1)

        @pl.when(g >= 2)
        def _():
            node_sum(g - 2)

        return carry

    lax.fori_loop(0, groups, group_step, 0)
    rep_sum(groups - 1)

    def early(g, carry):
        put_back(g)
        return carry

    lax.fori_loop(0, groups - 1, early, 0)
    if groups > 1:
        node_sum(groups - 2)
    node_sum(groups - 1)
    each(rr, lambda d: f_copy(d, mr).start())
    put_back(groups - 1)
    frecv[mr] = fsend[...]
    each(rr, lambda d: f_copy(d, rep_behind(d)).wait_recv())
    dw_ref[...] = frecv[...].reshape(rr * seg, width)

    peers(lambda d: g_copy(d, me).wait_send())
    peers(lambda d: t_copy(d, me).wait_send())

    def drain(g, carry):
        peers(lambda d: in_copy(g, d, me).wait_send())
        peers(lambda d: back_copy(g, d, me).wait_send())
        peers(lambda d: n_copy(g, d, me).wait_send())
        each(rr, lambda d: w_copy(g, d, mr).wait_send())
        return carry

    lax.fori_loop(0, groups, drain, 0)
    each(rr, lambda d: f_copy(d, mr).wait_send())


def local_kernel(queries, keys, values, grad_out, w_out, cluster_id):
    nn = lax.axis_size("nodes")
    rr = lax.axis_size("rep")
    rows, width = queries.shape[1:]
    bucket = rows // nn
    groups = width // HEAD_DIM // GROUP_HEADS
    gcols = width // groups
    seg = width // (nn * rr)
    norm_factor = 1.0 / math.sqrt(rr * nn * rows)
    low = jnp.bfloat16
    vmem = pl.BlockSpec(memory_space=pltpu.VMEM)
    dma = pltpu.SemaphoreType.DMA
    outs = pl.pallas_call(
        functools.partial(layer_kernel, nn, rr, groups, norm_factor),
        out_shape=[jax.ShapeDtypeStruct((rows, width), low)] * 3
        + [jax.ShapeDtypeStruct((rr * seg, width), low)],
        in_specs=[vmem] + [pl.BlockSpec(memory_space=pl.ANY)] * 5,
        out_specs=[vmem] * 4,
        scratch_shapes=[pltpu.VMEM((rows, width), low)] * 4 + [
            pltpu.VMEM((width, width), low),
            dma((5,)),
            pltpu.VMEM((rows, rows), low),
            pltpu.VMEM((rows, rows), low),
            pltpu.VMEM((nn, bucket, width), low),
            pltpu.VMEM((nn, bucket, width), low),
            pltpu.VMEM((nn, TAG_ROWS, TAG_LANES), low),
            pltpu.VMEM((nn, TAG_ROWS, TAG_LANES), low),
            pltpu.VMEM((groups, nn, 3, bucket, gcols), low),
            pltpu.VMEM((groups, nn, 3, bucket, gcols), low),
            pltpu.VMEM((rows, width), low),
            pltpu.VMEM((rows, rows), jnp.float32),
            pltpu.VMEM((rows, gcols), low),
            pltpu.VMEM((groups, nn, 3, bucket, gcols), low),
            pltpu.VMEM((groups, nn, 3, bucket, gcols), low),
            pltpu.VMEM((groups, rr, nn, seg, gcols), low),
            pltpu.VMEM((groups, rr, nn, seg, gcols), low),
            pltpu.VMEM((groups, nn, seg, gcols), low),
            pltpu.VMEM((groups, nn, seg, gcols), low),
            pltpu.VMEM((seg, width), low),
            pltpu.VMEM((rr, seg, width), low),
            dma((nn,)), dma((nn,)),
            dma((nn,)), dma((nn,)),
            dma((groups, nn)), dma((groups, nn)),
            dma((groups, nn)), dma((groups, nn)),
            dma((groups, rr)), dma((groups, rr)),
            dma((groups, nn)), dma((groups, nn)),
            dma((rr,)), dma((rr,)),
        ],
        compiler_params=pltpu.CompilerParams(
            collective_id=0, has_side_effects=True, vmem_limit_bytes=56 * 1024 * 1024
        ),
    )(cluster_id, queries[0], keys[0], values[0], grad_out[0], w_out)
    return (outs[0][None], outs[1][None], outs[2][None], outs[3].astype(jnp.float32))


def local(queries, keys, values, grad_out, w_out, cluster_id):
    nn, rr = lax.axis_size("nodes"), lax.axis_size("rep")
    rows, width = queries.shape[1:]
    heads = width // HEAD_DIM
    bucket_fits = rows // nn <= TAG_LANES
    fits = (
        rows % (16 * nn) == 0 and width % (16 * nn * rr) == 0 and heads % GROUP_HEADS == 0
        and CL_DEV <= TAG_ROWS and bucket_fits and nn > 1 and rr > 1
    )
    chosen = local_kernel if fits else local_plain
    return chosen(queries, keys, values, grad_out, w_out, cluster_id)


def solution(mesh):
    in_specs = (
        P("rep", "nodes", None),
        P("rep", "nodes", None),
        P("rep", "nodes", None),
        P("rep", "nodes", None),
        P(),
        P("rep", "nodes"),
    )
    out_specs = (
        P("rep", "nodes", None),
        P("rep", "nodes", None),
        P("rep", "nodes", None),
        P("nodes", None),
    )
    return jax.shard_map(local, mesh=mesh, in_specs=in_specs, out_specs=out_specs, check_vma=False)
```
